128 devices in a mesh: rows: 32 (over y_lo, z, x), cols: 4 (over y_hi, core).
Axes of the slice: x: 4, y: 4 (y_hi: 2, y_lo: 2; y = y_hi * 2 + y_lo), z: 4, core: 2. Of those that a mesh axis runs over, the one named last changes fastest.
Arguments:
- coords: float32 [2, 3, 262144], P(None, None, ('rows', 'cols')), may hold values from -6 to 6
- counts: bfloat16 [512, 8, 512, 512], P('rows', 'cols'), may hold values from 0 to 127, as said below
- tile_cols: int32 [512, 8], P('rows', 'cols'), may hold values from -1 to 511, as said below
- exponents: int32 [512, 8], P('rows', 'cols'), may hold values from 4 to 7
- chrom_starts: int32 [24], replicated, may hold values from 0 to 261632, as said below
Outputs:
- gradient: float32 [2, 3, 262144], P(None, None, ('rows', 'cols'))
The draws below stay inside these ranges and needn't reach their ends.
Inputs may be any that keep to these rules, and one draw needn't show every extreme that they name: `counts`: whole numbers. `tile_cols`: the live slots of one row tile and column group come first and name distinct tiles of that group; the group that holds the row tile's own index has all 2 slots live and names that index. `chrom_starts`: strictly rising, first entry 0, last entry 261632.
All inputs are finite; a program needn't handle non-finite values.
Results may differ from the reference program's by a relative error of at most 0.0003.
Values sent between devices are 32-bit elements; how exact they have to be, the bound alone decides.
No kernel may reach another device: no remote copies, remote signals or barrier semaphores. Data moves between devices by JAX's collectives and lax.ppermute only.
A program may use at most 448 MiB of HBM per device.

```python
import jax
import jax.numpy as jnp
from jax import lax

TILE = 512
TILES_PIECE = 4
SLOTS = 2
CHROMS = 24
TILE_ROWS = 512
BINS = 262144
N_ROWS = 32
N_COLS = 4


def draw_counts(key, part):
    values = jax.random.randint(key, (TILE_ROWS, N_COLS * SLOTS, TILE, TILE), 0, 128)
    values = values.at[0, 0, 0, 0].set(127)
    values = values.at[0, 0, 0, 1].set(0)
    return values.astype(jnp.float32).astype(jnp.bfloat16)


def draw_tile_cols(key, part):
    group_tiles = N_ROWS * TILES_PIECE
    key_score, key_live = jax.random.split(key)
    noise = jax.random.randint(key_score, (TILE_ROWS, N_COLS, group_tiles), 0, 65536)
    local_ids = jnp.arange(group_tiles, dtype=jnp.int32)
    group_ids = jnp.arange(N_COLS, dtype=jnp.int32)
    global_ids = (local_ids[None, :] // TILES_PIECE * N_COLS + group_ids[:, None]) * TILES_PIECE + local_ids[None, :] % TILES_PIECE
    row_ids = jnp.arange(TILE_ROWS, dtype=jnp.int32)
    spacing = jnp.abs(global_ids[None, :, :] - row_ids[:, None, None])
    closeness = jnp.maximum(4 - spacing, 0)
    scores = (noise + closeness * 65536) * group_tiles + local_ids[None, None, :]
    best_scores, picked = lax.top_k(scores, SLOTS)
    chosen = jnp.take_along_axis(jnp.broadcast_to(global_ids[None], scores.shape), picked, axis=2)
    live_count = jax.random.randint(key_live, (TILE_ROWS, N_COLS), 1, SLOTS + 1)
    home_group = row_ids // TILES_PIECE % N_COLS
    live_count = jnp.where(group_ids[None, :] == home_group[:, None], SLOTS, live_count)
    slot_ids = jnp.arange(SLOTS, dtype=jnp.int32)
    result = jnp.where(slot_ids[None, None, :] < live_count[:, :, None], chosen, -1)
    return result.reshape(TILE_ROWS, N_COLS * SLOTS).astype(jnp.int32)


def draw_chrom_starts(key, part):
    last_start = TILE_ROWS * TILE - TILE
    shuffled = jax.random.permutation(key, last_start - 1) + 1
    inner = jnp.sort(shuffled[:CHROMS - 2])
    return jnp.concatenate([jnp.zeros((1,), jnp.int32), inner.astype(jnp.int32), jnp.full((1,), last_start, jnp.int32)])


def place_ends(array, key, smallest, high):
    shape = array.shape
    index_at = [jax.random.randint(jax.random.fold_in(key, axis), (), 0, shape[axis]) for axis in range(len(shape))]
    array = array.at[tuple(index_at)].set(smallest)
    longest = shape.index(max(shape))
    index_at[longest] = (index_at[longest] + 1) % shape[longest]
    return array.at[tuple(index_at)].set(high)


def block_scale(rng, dims, cuts, smallest, top_value):
    level, own = 1.0, jax.random.fold_in(rng, 6)
    for position, blocks in cuts:
        draws = jnp.exp(jax.random.uniform(jax.random.fold_in(own, position), (blocks,), jnp.float32, smallest / len(cuts), top_value / len(cuts)))
        level = level * jnp.repeat(draws, dims[position] // blocks).reshape([-1 if axis == position else 1 for axis in range(len(dims))])
    return level


def scatter_about(key, dims, scale, bound, cuts=(), kind=jnp.bfloat16):
    array = scale * jax.random.normal(key, dims, jnp.float32)
    if cuts:
        array = array * block_scale(key, dims, cuts, -0.22, 0.18)
    return jnp.clip(array, -bound, bound).astype(kind)


def setup_inputs(seed: int = 0) -> dict:
    keys = jax.random.split(jax.random.key(seed), 6)
    return {
        "coords": scatter_about(keys[0], (2, 3, BINS), 1.0, 6.0, ((2, 128),), jnp.float32),
        "counts": draw_counts(jax.random.fold_in(keys[5], 71), 0),
        "tile_cols": draw_tile_cols(jax.random.fold_in(keys[5], 71), 0),
        "exponents": place_ends(jax.random.randint(keys[3], (TILE_ROWS, N_COLS * SLOTS), 4, 8), jax.random.fold_in(keys[3], 1), 4, 7).astype(jnp.int32),
        "chrom_starts": draw_chrom_starts(jax.random.fold_in(keys[5], 71), 0),
    }


BETA_SAME = 8.0
BETA_OTHER = 2.0
REPULSE = 24.0

def chrom_of(first_bin, width, starts):
    bin_ids = first_bin + lax.iota(jnp.int32, width)
    return lax.optimization_barrier(jnp.sum((bin_ids[:, None] >= starts[None, :]).astype(jnp.int32), axis=1)) - 1

def tile_terms(row_pos, col_pos, tile_counts, exponent, row_chrom, col_chrom, is_live):
    factor = jnp.exp2(-exponent.astype(jnp.float32))
    observed = tile_counts.astype(jnp.float32) * factor
    tile_size = tile_counts.shape[0]
    distance = jnp.zeros((row_pos.shape[0], tile_size, tile_size), jnp.float32)
    for component in range(3):
        offset = row_pos[:, component, :, None] - col_pos[:, component, None, :]
        distance = distance + offset * offset
    inverse = 1.0 / (1.0 + distance)
    affinity = jnp.where(row_chrom[:, None] == col_chrom[None, :], BETA_SAME, BETA_OTHER)
    expected = affinity * inverse * jnp.sqrt(inverse)
    slopes = 2.0 * (-1.5 * (expected - observed) * inverse - 2.0 * REPULSE * inverse * inverse * inverse) / tile_size
    slopes = slopes * is_live
    row_grad = row_pos * lax.optimization_barrier(jnp.sum(slopes, axis=2))[:, None, :] - jnp.einsum('tij,tcj->tci', slopes, col_pos, precision=lax.Precision.HIGHEST)
    col_grad = col_pos * lax.optimization_barrier(jnp.sum(slopes, axis=1))[:, None, :] - jnp.einsum('tij,tci->tcj', slopes, row_pos, precision=lax.Precision.HIGHEST)
    return (row_grad, col_grad)

def reference(coords, counts, tile_cols, exponents, chrom_starts):
    tile_size = counts.shape[2]
    tile_total = coords.shape[2] // tile_size
    blocked = coords.reshape(2, 3, tile_total, tile_size)
    tile_map = jax.vmap(tile_terms, in_axes=(None, 2, 0, 0, None, 0, 0), out_axes=(2, 2))
    chroms = jax.vmap(chrom_of, in_axes=(0, None, None))

    def row_step(gathered, tile_row):
        row_pos = blocked[:, :, tile_row]
        row_chrom = chrom_of(tile_row * tile_size, tile_size, chrom_starts)
        columns = tile_cols[tile_row]
        is_live = (columns >= 0).astype(jnp.float32)
        safe_cols = jnp.maximum(columns, 0).astype(jnp.int32)
        col_pos = blocked[:, :, safe_cols]
        col_chrom = chroms(safe_cols * tile_size, tile_size, chrom_starts)
        row_grad, col_grad = tile_map(row_pos, col_pos, counts[tile_row], exponents[tile_row], row_chrom, col_chrom, is_live)
        gathered = gathered.at[:, :, tile_row].add(lax.optimization_barrier(jnp.sum(row_grad, axis=2)))
        gathered = gathered.at[:, :, safe_cols].add(col_grad)
        return (gathered, None)
    result, _ = lax.scan(row_step, jnp.zeros(blocked.shape, jnp.float32), jnp.arange(tile_total, dtype=jnp.int32))
    return result.reshape(2, 3, tile_total * tile_size)
```

```python
import functools

import jax
import jax.numpy as jnp
from jax import lax
from jax.experimental import pallas as pl
from jax.experimental.pallas import tpu as pltpu
from jax.sharding import Mesh
from jax.sharding import PartitionSpec as P

BETA_SAME = 8.0
BETA_OTHER = 2.0
REPULSE = 24.0
ALPHA = (4.0 / 3.0 * REPULSE) ** -0.5
B_SAME = BETA_SAME * ALPHA**1.5
B_OTHER = BETA_OTHER * ALPHA**1.5

ROWS = ("yl", "z", "x")
COLS = ("yh", "c")
LANES = 128
CHUNK = 128


def split3(x):
    hi = x.astype(jnp.bfloat16).astype(jnp.float32)
    rest = x - hi
    mid = rest.astype(jnp.bfloat16).astype(jnp.float32)
    return hi, mid, rest - mid


def unpack_tile(ref, tile, trial, quarters):
    parts = [ref[tile, pl.ds(trial * 3 * quarters + 3 * q, 3), :] for q in range(quarters)]
    pos = jnp.concatenate(parts, axis=1)
    return jnp.concatenate([pos, jnp.zeros((5, pos.shape[1]), jnp.float32)], axis=0)


def row_ids(width):
    return lax.broadcasted_iota(jnp.int32, (8, width), 0)


def put(base, values, first, width):
    ids = row_ids(width)
    for n, value in enumerate(values):
        base = jnp.where(ids == first + n, value, base)
    return base


def moment_rows(hi, mid, low):
    width = hi.shape[1]
    top = put(hi, [1.0], 3, width) + pltpu.roll(mid, 4, 0)
    return jnp.concatenate([top, low], axis=0).astype(jnp.bfloat16)


def distance_rows(pos, is_row):
    width = pos.shape[1]
    norm = ALPHA * jnp.sum(pos * pos, axis=0, keepdims=True)
    if is_row:
        hi, mid, low = split3(pos)
        first = put(hi, split3(norm), 3, width)
        second = put(mid, [1.0, 1.0, 1.0], 3, width)
        groups = [first, second, low, hi, mid, hi]
    else:
        hi, mid, low = split3((-2.0 * ALPHA) * pos)
        first = put(hi, [1.0, 1.0, 1.0], 3, width)
        second = put(hi, split3(norm + ALPHA), 3, width)
        groups = [first, second, hi, mid, mid, low]
    return jnp.concatenate(groups, axis=0)


def finish(total, pos):
    total = total[0:8] + total[8:16]
    total = total + pltpu.roll(total, 4, 0)
    return pos * total[3:4] - total


def add_tile(ref, tile, trial, grad, scale, quarters):
    for q in range(quarters):
        rows = pl.ds(trial * 3 * quarters + 3 * q, 3)
        ref[tile, rows, :] += scale * grad[0:3, q * LANES : (q + 1) * LANES]


def chrom_row(starts, first_bin, width):
    bins = first_bin + lax.broadcasted_iota(jnp.int32, (8, width), 1)
    total = jnp.zeros((8, width), jnp.int32)
    for n in range(starts.shape[0]):
        total += (bins >= starts[n]).astype(jnp.int32)
    return total


def kernel(
    group, columns, exponents, starts, row_ref, col_ref, counts_hbm,
    row_out, col_out, counts, sems, row_dist, row_moment, row_total,
):
    row_tiles, slots, tile_size = counts_hbm.shape[0], counts_hbm.shape[1], counts_hbm.shape[2]
    quarters = tile_size // LANES
    piece = row_tiles // group[2]
    scale = 3.0 * ALPHA / tile_size

    def copy(n):
        return pltpu.make_async_copy(counts_hbm.at[n // slots, n % slots], counts.at[n], sems.at[n])

    def start(n, carry):
        copy(n).start()
        return carry

    lax.fori_loop(0, row_tiles * slots, start, 0)
    row_out[...] = jnp.zeros_like(row_out)
    col_out[...] = jnp.zeros_like(col_out)

    def row_step(i, carry):
        row_pos = [unpack_tile(row_ref, i, t, quarters) for t in range(2)]
        for t in range(2):
            row_dist[t] = distance_rows(row_pos[t], True).T.astype(jnp.bfloat16)
            row_moment[t] = moment_rows(*split3(row_pos[t]))
            row_total[t] = jnp.zeros((16, tile_size), jnp.float32)
        row_tile = group[0] * row_tiles + i
        row_chrom = chrom_row(starts, row_tile * tile_size, tile_size)
        row_chrom = row_chrom.astype(jnp.float32).T[:, 0:1]

        for k in range(slots):
            n = i * slots + k
            copy(n).wait()
            column = columns[i, k]

            @pl.when(column >= 0)
            def _():
                local = column // (piece * group[2]) * piece + column % piece
                col_pos = [unpack_tile(col_ref, local, t, quarters) for t in range(2)]
                col_dist = [distance_rows(col_pos[t], False).astype(jnp.bfloat16) for t in range(2)]
                col_moment = [moment_rows(*split3(col_pos[t])) for t in range(2)]
                col_chrom = chrom_row(starts, column * tile_size, tile_size)[0:1].astype(jnp.float32)
                factor = jnp.exp2(jnp.full((1, LANES), -exponents[i, k], jnp.int32).astype(jnp.float32))[0:1, 0:1]
                col_total = [jnp.zeros((16, tile_size), jnp.float32) for t in range(2)]
                for c in range(tile_size // CHUNK):
                    rows = slice(c * CHUNK, (c + 1) * CHUNK)
                    observed = counts[n, rows, :].astype(jnp.float32) * factor
                    beta = jnp.where(row_chrom[rows] == col_chrom, B_SAME, B_OTHER)
                    for t in range(2):
                        s = jnp.dot(row_dist[t, rows, :], col_dist[t], preferred_element_type=jnp.float32)
                        r = lax.rsqrt(s)
                        r2 = r * r
                        w = r2 * (observed - r2 * (r * (beta + r)))
                        w = w.astype(jnp.bfloat16)
                        row_total[t, :, rows] += lax.dot_general(
                            col_moment[t], w, (((1,), (1,)), ((), ())), preferred_element_type=jnp.float32
                        )
                        col_total[t] += jnp.dot(row_moment[t, :, rows], w, preferred_element_type=jnp.float32)
                for t in range(2):
                    add_tile(col_out, local, t, finish(col_total[t], col_pos[t]), scale, quarters)

        for t in range(2):
            add_tile(row_out, i, t, finish(row_total[t], row_pos[t]), scale, quarters)
        return carry

    lax.fori_loop(0, row_tiles, row_step, 0)


def tile_gradients(group, columns, exponents, starts, row_pos, col_pos, counts):
    row_tiles, slots, tile_size = counts.shape[0], counts.shape[1], counts.shape[2]
    smem = pl.BlockSpec(memory_space=pltpu.SMEM)
    vmem = pl.BlockSpec(memory_space=pltpu.VMEM)
    return pl.pallas_call(
        kernel,
        out_shape=[
            jax.ShapeDtypeStruct(row_pos.shape, jnp.float32),
            jax.ShapeDtypeStruct(col_pos.shape, jnp.float32),
        ],
        in_specs=[smem] * 4 + [vmem] * 2 + [pl.BlockSpec(memory_space=pl.ANY)],
        out_specs=[vmem, vmem],
        scratch_shapes=[
            pltpu.VMEM((row_tiles * slots, tile_size, tile_size), jnp.bfloat16),
            pltpu.SemaphoreType.DMA((row_tiles * slots,)),
            pltpu.VMEM((2, tile_size, 48), jnp.bfloat16),
            pltpu.VMEM((2, 16, tile_size), jnp.bfloat16),
            pltpu.VMEM((2, 16, tile_size), jnp.float32),
        ],
        compiler_params=pltpu.CompilerParams(vmem_limit_bytes=48 * 1024 * 1024),
        name="tile_gradients",
    )(group, columns, exponents, starts, row_pos, col_pos, counts)


def body(coords, counts, tile_cols, exponents, chrom_starts):
    row_tiles, tile_size = counts.shape[0], counts.shape[2]
    width = coords.shape[2]
    tiles, quarters = width // tile_size, tile_size // LANES
    n_rows, n_cols = lax.axis_size(ROWS), lax.axis_size(COLS)
    local = coords.reshape(2, 3, tiles, quarters, LANES).transpose(2, 0, 3, 1, 4)
    local = local.reshape(tiles * 6 * quarters, LANES)
    row_pos = lax.all_gather(local, COLS, axis=0, tiled=True)
    col_pos = jnp.broadcast_to(local[None], (n_rows,) + local.shape)
    col_pos = lax.all_to_all(col_pos, ROWS, 0, 0, tiled=True)
    group = jnp.stack([lax.axis_index(ROWS), lax.axis_index(COLS), jnp.int32(n_cols)])
    row_part, col_part = tile_gradients(
        group, tile_cols, exponents, chrom_starts,
        row_pos.reshape(row_tiles, 6 * quarters, LANES),
        col_pos.reshape(n_rows * tiles, 6 * quarters, LANES),
        counts,
    )
    col_part = lax.all_to_all(col_part.reshape((n_rows,) + local.shape), ROWS, 0, 0, tiled=True)
    row_part = lax.all_to_all(row_part.reshape((n_cols,) + local.shape), COLS, 0, 0, tiled=True)
    grad = jnp.sum(col_part, axis=0) + jnp.sum(row_part, axis=0)
    grad = grad.reshape(tiles, 2, quarters, 3, LANES).transpose(1, 3, 0, 2, 4)
    return grad.reshape(2, 3, width)


def solution(mesh):
    fine = Mesh(mesh.devices.reshape(2, 4, 4, 2, 2), ROWS + COLS)
    placed = (
        P(None, None, ROWS + COLS),
        P(ROWS, COLS, None, None),
        P(ROWS, COLS),
        P(ROWS, COLS),
        P(),
    )
    return jax.shard_map(
        body, mesh=fine, in_specs=placed, out_specs=P(None, None, ROWS + COLS), check_vma=False
    )
```

```python
import functools

import jax
import jax.numpy as jnp
from jax import lax
from jax.experimental import pallas as pl
from jax.experimental.pallas import tpu as pltpu
from jax.sharding import Mesh
from jax.sharding import PartitionSpec as P

BETA_SAME = 8.0
BETA_OTHER = 2.0
REPULSE = 24.0
EXPONENTS = (4, 5, 6, 7)
FACTORS = tuple(2.0**-e for e in EXPONENTS)
ALPHAS = tuple((f / (4.0 / 3.0 * REPULSE)) ** 0.5 for f in FACTORS)
HALF_ROOT = 0.5**0.5
ODD = tuple(e % 2 == 0 for e in EXPONENTS)
POWERS = tuple(2.0 ** -((e + 5) // 2) for e in EXPONENTS)
SLOPES = tuple(a**1.5 / f for a, f in zip(ALPHAS, FACTORS))
SCALES = tuple(3.0 * a * f for a, f in zip(ALPHAS, FACTORS))

ROWS = ("yl", "z", "x")
COLS = ("yh", "c")
LANES = 128
STEP = 32
GROUPS = 8
MOMENTS = 32


def pick(exponent, table):
    value = jnp.float32(table[-1])
    for e, entry in zip(EXPONENTS[-2::-1], table[-2::-1]):
        value = jnp.where(exponent <= e, jnp.float32(entry), value)
    return value


def split3(x):
    hi = x.astype(jnp.bfloat16).astype(jnp.float32)
    rest = x - hi
    mid = rest.astype(jnp.bfloat16).astype(jnp.float32)
    return hi, mid, rest - mid


def spread(tile):
    parts = [tile[6 * q : 6 * q + 6] for q in range(tile.shape[0] // 6)]
    wide = jnp.concatenate(parts, axis=1)
    return jnp.concatenate([wide, jnp.zeros((2, wide.shape[1]), jnp.float32)], axis=0)


def fold(wide):
    parts = [wide[0:6, q * LANES : (q + 1) * LANES] for q in range(wide.shape[1] // LANES)]
    return jnp.concatenate(parts, axis=0)


def row_ids(width):
    return lax.broadcasted_iota(jnp.int32, (8, width), 0)


def norms(pos):
    square = pos * pos
    return square + pltpu.roll(square, 7, 0) + pltpu.roll(square, 6, 0)


def moment_rows(hi, mid, low):
    ids = row_ids(hi.shape[1])
    top = jnp.where(ids == 6, 1.0, hi)
    return jnp.concatenate([top, mid, low, jnp.zeros_like(low)], axis=0).astype(jnp.bfloat16)


def norm_rows(norm):
    ids = row_ids(norm.shape[1])
    hi, mid, low = split3(norm)
    first = (ids == 0) | (ids == 3)
    second = (ids == 1) | (ids == 4)
    rows = jnp.where(first, hi, jnp.where(second, pltpu.roll(mid, 1, 0), pltpu.roll(low, 2, 0)))
    return rows, ids


def row_operand(pos):
    hi, mid, low = split3(pos)
    norm = norms(pos)
    rows, ids = norm_rows(norm)
    rows = jnp.where(ids >= 6, 1.0, rows)
    scaled, _ = norm_rows(norm * HALF_ROOT)
    scaled = jnp.where(ids == 6, 1.0, jnp.where(ids == 7, 0.0, scaled))
    operand = jnp.concatenate([hi, hi, mid, hi, mid, low, rows, scaled], axis=0)
    return operand, moment_rows(hi, mid, low)


def column_operand(pos, exponent):
    alpha = pick(exponent, ALPHAS)
    even = pick(exponent, [0.0 if odd else p for odd, p in zip(ODD, POWERS)])
    odd = pick(exponent, [p if odd else 0.0 for odd, p in zip(ODD, POWERS)])
    hi, mid, low = split3(pos * (-2.0 * alpha))
    norm = split3(alpha * (norms(pos) + 1.0))
    ids = row_ids(pos.shape[1])
    operands = []
    for t in range(2):
        mine = (ids < 3) if t == 0 else ((ids >= 3) & (ids < 6))
        h, m, l = [jnp.where(mine, x, 0.0) for x in (hi, mid, low)]
        up = [pltpu.roll(norm[n], (6 + n % 2 - 3 * t) % 8, 0) for n in range(3)]
        first = jnp.where(ids == 6, up[0], jnp.where(ids == 7, up[1], jnp.where(mine, even, 0.0)))
        second = jnp.where(ids == 6, up[2], jnp.where(mine, odd, 0.0))
        operands.append(jnp.concatenate([h, m, h, l, m, h, first, second], axis=0).astype(jnp.bfloat16))
    return operands, moment_rows(hi, mid, low)


def gather_moments(parts):
    sums = [p[0:8] + p[8:16] + p[16:24] for p in parts]
    ids = row_ids(sums[0].shape[1])
    return jnp.where(ids < 3, sums[0], sums[1]), jnp.where(ids < 3, sums[0][6:7], sums[1][6:7])


def chrom_row(starts, first_bin, width):
    bins = first_bin + lax.broadcasted_iota(jnp.int32, (8, width), 1)
    total = jnp.zeros((8, width), jnp.int32)
    for n in range(starts.shape[0]):
        total += (bins >= starts[n]).astype(jnp.int32)
    return total.astype(jnp.float32)


def kernel(window, group, columns, exponents, starts, *refs):
    if window:
        row_ref, counts_hbm, row_out = refs[:3]
        col_ref, col_out = row_ref, row_out
        scratch = refs[3:]
    else:
        row_ref, col_ref, counts_hbm, row_out, col_out = refs[:5]
        scratch = refs[5:]
    counts, sems, live, low_bin, high_bin, row_dist, row_mom, col_dist, col_mom, slopes, dist, half_row, half_col = scratch
    row_tiles, slots, tile_size = counts_hbm.shape[0], counts_hbm.shape[1], counts_hbm.shape[2]
    me, n_cols = group[1], group[2]
    piece = row_tiles // n_cols
    half = tile_size // 2
    row_first = group[0] * row_tiles
    contract_last = (((1,), (1,)), ((), ()))

    def copy(n):
        return pltpu.make_async_copy(counts_hbm.at[n // slots, n % slots], counts.at[n], sems.at[n])

    def start(n, total):
        i = n // slots
        column = columns[i, n % slots]
        is_own = column == row_first + i
        is_live = is_own if window else ((column >= 0) & jnp.logical_not(is_own))
        live[total] = n

        @pl.when(is_live)
        def _():
            copy(n).start()

        return total + is_live.astype(jnp.int32)

    live[0] = 0
    total = lax.fori_loop(0, row_tiles * slots, start, jnp.int32(0))
    row_out[...] = jnp.zeros_like(row_out)
    if not window:
        col_out[...] = jnp.zeros_like(col_out)
    slopes[1] = jnp.zeros(slopes.shape[1:], slopes.dtype)
    half_row[...] = jnp.zeros_like(half_row)
    half_col[...] = jnp.zeros_like(half_col)

    def prepare_row(i, carry):
        operand, moments = row_operand(spread(row_ref[i]))
        row_dist[i] = operand.T.astype(jnp.bfloat16)
        row_mom[i] = moments
        first = (row_first + (i // piece + me) % n_cols * piece + i % piece) * tile_size
        low, high = jnp.int32(0), jnp.int32(2**30)
        for n in range(starts.shape[0]):
            low = jnp.where(starts[n] <= first, starts[n], low)
        for n in range(starts.shape[0] - 1, -1, -1):
            high = jnp.where(starts[n] > first, starts[n], high)
        low_bin[i] = low
        high_bin[i] = high
        return carry

    lax.fori_loop(0, row_ref.shape[0], prepare_row, 0)

    def place(n):
        n = live[jnp.clip(n, 0, jnp.maximum(total - 1, 0))]
        i, k = n // slots, n % slots
        column = jnp.maximum(columns[i, k], 0)
        local = column // (piece * n_cols) * piece + column % piece
        if window:
            local = jnp.where(columns[i, k] == row_first + i, column % piece, 0)
        row = (i // piece - me + n_cols) % n_cols * piece + i % piece
        return n, jnp.minimum(row, row_ref.shape[0] - 1), column, local, exponents[i, k]

    def prepare_column(n):
        _, _, _, local, exponent = place(n)
        operands, moments = column_operand(spread(col_ref[local]), exponent)
        for t in range(2):
            col_dist[t] = operands[t]
        col_mom[1] = moments

    def distances(n, part):
        i = place(n)[1]
        for t in range(2):
            dist[part, t] = jnp.dot(
                row_dist[i, part * half : (part + 1) * half, :], col_dist[t], preferred_element_type=jnp.float32
            )

    def multiply(n, part):
        i = place(n)[1]
        rows = slice(part * half, (part + 1) * half)
        for t in range(2):
            w = slopes[part, t]
            half_row[t, :, rows] = lax.dot_general(
                col_mom[0], w, contract_last, preferred_element_type=jnp.float32
            )
            value = jnp.dot(row_mom[i, :, rows], w, preferred_element_type=jnp.float32)
            if part == 0:
                half_col[t] = value
            else:
                half_col[t] += value

    def finish(n):
        _, i, _, local, exponent = place(n)
        scale = pick(exponent, SCALES) * (1.0 / tile_size)
        back = pick(exponent, [-0.5 / a for a in ALPHAS])
        moment, weight = gather_moments([half_row[0], half_row[1]])
        row_out[i] += fold(scale * (spread(row_ref[i]) * weight - back * moment))
        moment, weight = gather_moments([half_col[0], half_col[1]])
        col_out[local] += fold(scale * (spread(col_ref[local]) * weight - moment))

    def elementwise(n, part, uniform):
        n, i, column, _, exponent = place(n)
        slope = pick(exponent, SLOPES)
        first = column * tile_size
        if uniform:
            bins = first + lax.broadcasted_iota(jnp.int32, (8, tile_size), 1)
            same = (bins >= low_bin[i]) & (bins < high_bin[i])
            beta = jnp.where(same, BETA_SAME * slope, BETA_OTHER * slope)
            beta = jnp.concatenate([beta] * (STEP // 8), axis=0)
        else:
            row_chrom = chrom_row(starts, (row_first + n // slots) * tile_size + part * half, half).T[:, 0:1]
            col_chrom = chrom_row(starts, first, tile_size)[0:1]
        for c in range(half // STEP):
            rows = slice(c * STEP, (c + 1) * STEP)
            observed = counts[n, part * half + c * STEP : part * half + (c + 1) * STEP, :].astype(jnp.float32)
            if not uniform:
                beta = jnp.where(row_chrom[rows] == col_chrom, BETA_SAME * slope, BETA_OTHER * slope)
            for t in range(2):
                r = lax.rsqrt(dist[part, t, rows, :])
                r2 = r * r
                w = r2 * (observed - r2 * (r * (beta + r)))
                slopes[part, t, rows, :] = w.astype(jnp.bfloat16)

    def step(n, uniform):
        distances(n, 1)
        elementwise(n, 0, uniform)
        multiply(n - 1, 1)
        finish(n - 1)
        col_mom[0] = col_mom[1]
        prepare_column(n + 1)
        distances(n + 1, 0)
        elementwise(n, 1, uniform)
        multiply(n, 0)

    prepare_column(0)
    distances(0, 0)
    col_mom[0] = jnp.zeros_like(col_mom[1])

    def loop(n, carry):
        slot, i, _, _, _ = place(n)
        copy(slot).wait()
        uniform = high_bin[i] >= (row_first + slot // slots + 1) * tile_size

        @pl.when(uniform)
        def _():
            step(n, True)

        @pl.when(jnp.logical_not(uniform))
        def _():
            step(n, False)

        return carry

    lax.fori_loop(0, total, loop, 0)
    multiply(total - 1, 1)
    finish(total - 1)


def scratch_of(counts, rows):
    row_tiles, slots, tile_size = counts.shape[0], counts.shape[1], counts.shape[2]
    half = tile_size // 2
    return [
        pltpu.VMEM((row_tiles * slots, tile_size, tile_size), jnp.bfloat16),
        pltpu.SemaphoreType.DMA((row_tiles * slots,)),
        pltpu.SMEM((row_tiles * slots + 1,), jnp.int32),
        pltpu.SMEM((rows,), jnp.int32),
        pltpu.SMEM((rows,), jnp.int32),
        pltpu.VMEM((rows, tile_size, 8 * GROUPS), jnp.bfloat16),
        pltpu.VMEM((rows, MOMENTS, tile_size), jnp.bfloat16),
        pltpu.VMEM((2, 8 * GROUPS, tile_size), jnp.bfloat16),
        pltpu.VMEM((2, MOMENTS, tile_size), jnp.bfloat16),
        pltpu.VMEM((2, 2, half, tile_size), jnp.bfloat16),
        pltpu.VMEM((2, 2, half, tile_size), jnp.float32),
        pltpu.VMEM((2, MOMENTS, tile_size), jnp.float32),
        pltpu.VMEM((2, MOMENTS, tile_size), jnp.float32),
    ]


SMEM = pl.BlockSpec(memory_space=pltpu.SMEM)
VMEM = pl.BlockSpec(memory_space=pltpu.VMEM)
PARAMS = pltpu.CompilerParams(vmem_limit_bytes=44 * 1024 * 1024)


def own_gradients(group, columns, exponents, starts, own_pos, counts):
    return pl.pallas_call(
        functools.partial(kernel, True),
        out_shape=jax.ShapeDtypeStruct(own_pos.shape, jnp.float32),
        in_specs=[SMEM] * 4 + [VMEM, pl.BlockSpec(memory_space=pl.ANY)],
        out_specs=VMEM,
        scratch_shapes=scratch_of(counts, own_pos.shape[0]),
        compiler_params=PARAMS,
        name="own_gradients",
    )(group, columns, exponents, starts, own_pos, counts)


def tile_gradients(group, columns, exponents, starts, row_pos, col_pos, counts):
    return pl.pallas_call(
        functools.partial(kernel, False),
        out_shape=[
            jax.ShapeDtypeStruct(row_pos.shape, jnp.float32),
            jax.ShapeDtypeStruct(col_pos.shape, jnp.float32),
        ],
        in_specs=[SMEM] * 4 + [VMEM] * 2 + [pl.BlockSpec(memory_space=pl.ANY)],
        out_specs=[VMEM, VMEM],
        scratch_shapes=scratch_of(counts, row_pos.shape[0]),
        compiler_params=PARAMS,
        name="tile_gradients",
    )(group, columns, exponents, starts, row_pos, col_pos, counts)


def body(coords, counts, tile_cols, exponents, chrom_starts):
    row_tiles, tile_size = counts.shape[0], counts.shape[2]
    width = coords.shape[2]
    tiles, quarters = width // tile_size, tile_size // LANES
    n_rows, n_cols = lax.axis_size(ROWS), lax.axis_size(COLS)
    local = coords.reshape(2, 3, tiles, quarters, LANES).transpose(2, 3, 0, 1, 4)
    local = local.reshape(tiles, 6 * quarters, LANES)
    col_pos = jnp.broadcast_to(local[None], (n_rows,) + local.shape)
    col_pos = lax.all_to_all(col_pos, ROWS, 0, 0, tiled=True).reshape((n_rows * tiles,) + local.shape[1:])
    pieces = [
        lax.ppermute(local, COLS, [((g + shift) % n_cols, g) for g in range(n_cols)]) for shift in range(1, n_cols)
    ]
    row_pos = jnp.concatenate([local] + pieces, axis=0)
    group = jnp.stack([lax.axis_index(ROWS), lax.axis_index(COLS), jnp.int32(n_cols)])
    own_part = own_gradients(group, tile_cols, exponents, chrom_starts, local, counts)
    row_part, col_part = tile_gradients(group, tile_cols, exponents, chrom_starts, row_pos, col_pos, counts)
    col_part = lax.all_to_all(col_part.reshape((n_rows,) + local.shape), ROWS, 0, 0, tiled=True)
    row_sum = own_part + row_part[:tiles]
    for shift in range(1, n_cols):
        piece = row_part[shift * tiles : (shift + 1) * tiles]
        row_sum += lax.ppermute(piece, COLS, [(g, (g + shift) % n_cols) for g in range(n_cols)])
    grad = jnp.sum(col_part, axis=0) + row_sum
    grad = grad.reshape(tiles, quarters, 2, 3, LANES).transpose(2, 3, 0, 1, 4)
    return grad.reshape(2, 3, width)


def solution(mesh):
    fine = Mesh(mesh.devices.reshape(2, 4, 4, 2, 2), ROWS + COLS)
    placed = (
        P(None, None, ROWS + COLS),
        P(ROWS, COLS, None, None),
        P(ROWS, COLS),
        P(ROWS, COLS),
        P(),
    )
    return jax.shard_map(
        body, mesh=fine, in_specs=placed, out_specs=P(None, None, ROWS + COLS), check_vma=False
    )
```

```python
import functools

import jax
import jax.numpy as jnp
from jax import lax
from jax.experimental import pallas as pl
from jax.experimental.pallas import tpu as pltpu
from jax.sharding import Mesh
from jax.sharding import PartitionSpec as P

BETA_SAME = 8.0
BETA_OTHER = 2.0
REPULSE = 24.0
EXPONENTS = (4, 5, 6, 7)
FACTORS = tuple(2.0**-e for e in EXPONENTS)
ALPHAS = tuple((f / (4.0 / 3.0 * REPULSE)) ** 0.5 for f in FACTORS)
HALF_ROOT = 0.5**0.5
ODD = tuple(e % 2 == 0 for e in EXPONENTS)
POWERS = tuple(2.0 ** -((e + 5) // 2) for e in EXPONENTS)
SLOPES = tuple(a**1.5 / f for a, f in zip(ALPHAS, FACTORS))
SCALES = tuple(3.0 * a * f for a, f in zip(ALPHAS, FACTORS))

ROWS = ("yl", "z", "x")
COLS = ("yh", "c")
LANES = 128
STEP = 32
GROUPS = 4
MOMENTS = 16
AHEAD = 6
TOGETHER = 4


def pick(exponent, table):
    value = jnp.float32(table[-1])
    for e, entry in zip(EXPONENTS[-2::-1], table[-2::-1]):
        value = jnp.where(exponent <= e, jnp.float32(entry), value)
    return value


def split3(x):
    hi = x.astype(jnp.bfloat16).astype(jnp.float32)
    rest = x - hi
    mid = rest.astype(jnp.bfloat16).astype(jnp.float32)
    return hi, mid, rest - mid


def spread(tile):
    parts = [tile[6 * q : 6 * q + 6] for q in range(tile.shape[0] // 6)]
    wide = jnp.concatenate(parts, axis=1)
    return jnp.concatenate([wide, jnp.zeros((2, wide.shape[1]), jnp.float32)], axis=0)


def fold(wide):
    parts = [wide[0:6, q * LANES : (q + 1) * LANES] for q in range(wide.shape[1] // LANES)]
    return jnp.concatenate(parts, axis=0)


def row_ids(width):
    return lax.broadcasted_iota(jnp.int32, (8, width), 0)


def norms(pos):
    square = pos * pos
    return square + pltpu.roll(square, 7, 0) + pltpu.roll(square, 6, 0)


def own_rows(low, high, trial):
    ids = row_ids(low.shape[1])
    if trial == 0:
        high = pltpu.roll(high, 3, 0)
    else:
        low = pltpu.roll(low, 5, 0)
    return jnp.where(ids < 3, low, jnp.where(ids < 6, high, 0.0))


def moment_rows(hi, mid, low, trial):
    ids = row_ids(hi.shape[1])
    if trial == 1:
        hi, low = pltpu.roll(hi, 5, 0), pltpu.roll(low, 5, 0)
    mid = pltpu.roll(mid, 4 - 3 * trial, 0)
    top = jnp.where(ids < 3, hi, jnp.where(ids == 3, 1.0, jnp.where(ids < 7, mid, 0.0)))
    return jnp.concatenate([top, jnp.where(ids < 3, low, 0.0)], axis=0).astype(jnp.bfloat16)


def norm_rows(norm):
    ids = row_ids(norm.shape[1])
    hi, mid, low = split3(norm)
    first = (ids == 0) | (ids == 3)
    second = (ids == 1) | (ids == 4)
    rows = jnp.where(first, hi, jnp.where(second, pltpu.roll(mid, 1, 0), pltpu.roll(low, 2, 0)))
    return rows, ids


def row_operand(pos):
    hi, mid, low = split3(pos)
    norm = norms(pos)
    rows, ids = norm_rows(norm)
    scaled, _ = norm_rows(norm * HALF_ROOT)
    operands, moments = [], []
    for t in range(2):
        first = jnp.where(ids >= 6, 1.0, own_rows(hi, hi, t))
        second = jnp.where(ids == 6, 1.0, own_rows(mid, hi, t))
        operand = jnp.concatenate([first, second, own_rows(mid, low, t), own_rows(rows, scaled, t)], axis=0)
        operands.append(operand.astype(jnp.bfloat16))
        moments.append(moment_rows(hi, mid, low, t))
    return operands, moments


def column_operand(pos, exponent):
    alpha = pick(exponent, ALPHAS)
    even = pick(exponent, [0.0 if odd else p for odd, p in zip(ODD, POWERS)])
    odd = pick(exponent, [p if odd else 0.0 for odd, p in zip(ODD, POWERS)])
    hi, mid, low = split3(pos * (-2.0 * alpha))
    norm = split3(alpha * (norms(pos) + 1.0))
    ids = row_ids(pos.shape[1])
    powers = jnp.where(ids < 3, even, jnp.where(ids < 6, odd, 0.0))
    operands, moments = [], []
    for t in range(2):
        up = [pltpu.roll(norm[n], (6 + n % 2 - 3 * t) % 8, 0) for n in range(3)]
        first = jnp.where(ids == 6, up[0], jnp.where(ids == 7, up[1], own_rows(hi, mid, t)))
        second = jnp.where(ids == 6, up[2], own_rows(hi, low, t))
        operand = jnp.concatenate([first, second, own_rows(mid, hi, t), powers], axis=0)
        operands.append(operand.astype(jnp.bfloat16))
        moments.append(moment_rows(hi, mid, low, t))
    return operands, moments


def gather_moments(parts):
    sums = [p[0:8] + p[8:16] for p in parts]
    sums = [p + pltpu.roll(p, 4, 0) for p in sums]
    ids = row_ids(sums[0].shape[1])
    moment = jnp.where(ids < 3, sums[0], pltpu.roll(sums[1], 3, 0))
    return moment, jnp.where(ids < 3, sums[0][3:4], sums[1][3:4])


def chrom_row(starts, first_bin, width):
    bins = first_bin + lax.broadcasted_iota(jnp.int32, (8, width), 1)
    total = jnp.zeros((8, width), jnp.int32)
    for n in range(starts.shape[0]):
        total += (bins >= starts[n]).astype(jnp.int32)
    return total.astype(jnp.float32)


def kernel(window, group, columns, exponents, starts, *refs):
    if window:
        row_ref, counts_hbm, row_out = refs[:3]
        col_ref, col_out = row_ref, row_out
        scratch = refs[3:]
    else:
        row_ref, col_ref, counts_hbm, row_out, col_out = refs[:5]
        scratch = refs[5:]
    counts, sems, live, low_bin, high_bin, row_dist, row_mom, col_dist, col_mom, slopes, dist, half_row, half_col = scratch
    row_tiles, slots, tile_size = counts_hbm.shape[0], counts_hbm.shape[1], counts_hbm.shape[2]
    me, n_cols = group[1], group[2]
    piece = row_tiles // n_cols
    half = tile_size // 2
    row_first = group[0] * row_tiles
    contract_last = (((1,), (1,)), ((), ()))

    def copy(n):
        return pltpu.make_async_copy(counts_hbm.at[n // slots, n % slots], counts.at[n], sems.at[n])

    def start(n, total):
        i = n // slots
        column = columns[i, n % slots]
        is_own = column == row_first + i
        is_live = is_own if window else ((column >= 0) & jnp.logical_not(is_own))
        live[total] = n

        @pl.when(is_live & (total < AHEAD))
        def _():
            copy(n).start()

        return total + is_live.astype(jnp.int32)

    live[0] = 0
    total = lax.fori_loop(0, row_tiles * slots, start, jnp.int32(0))
    row_out[...] = jnp.zeros_like(row_out)
    if not window:
        col_out[...] = jnp.zeros_like(col_out)
    slopes[1] = jnp.zeros(slopes.shape[1:], slopes.dtype)
    half_row[...] = jnp.zeros_like(half_row)
    half_col[...] = jnp.zeros_like(half_col)

    def prepare_row(i, carry):
        operands, moments = row_operand(spread(row_ref[i]))
        for t in range(2):
            row_dist[i, t] = operands[t].T
            row_mom[i, t] = moments[t]
        first = (row_first + (i // piece + me) % n_cols * piece + i % piece) * tile_size
        low, high = jnp.int32(0), jnp.int32(2**30)
        for n in range(starts.shape[0]):
            low = jnp.where(starts[n] <= first, starts[n], low)
        for n in range(starts.shape[0] - 1, -1, -1):
            high = jnp.where(starts[n] > first, starts[n], high)
        low_bin[i] = low
        high_bin[i] = high
        return carry

    lax.fori_loop(0, row_ref.shape[0], prepare_row, 0, unroll=4)

    def place(n):
        n = live[jnp.clip(n, 0, jnp.maximum(total - 1, 0))]
        i, k = n // slots, n % slots
        column = jnp.maximum(columns[i, k], 0)
        local = column // (piece * n_cols) * piece + column % piece
        if window:
            local = jnp.where(columns[i, k] == row_first + i, column % piece, 0)
        row = (i // piece - me + n_cols) % n_cols * piece + i % piece
        return n, jnp.minimum(row, row_ref.shape[0] - 1), column, local, exponents[i, k]

    def prepare_column(n):
        _, _, _, local, exponent = place(n)
        operands, moments = column_operand(spread(col_ref[local]), exponent)
        for t in range(2):
            col_dist[t] = operands[t]
            col_mom[1, t] = moments[t]

    def distances(n, part):
        i = place(n)[1]
        for t in range(2):
            dist[part, t] = jnp.dot(
                row_dist[i, t, part * half : (part + 1) * half, :], col_dist[t], preferred_element_type=jnp.float32
            )

    def multiply(n, part):
        i = place(n)[1]
        rows = slice(part * half, (part + 1) * half)
        for t in range(2):
            w = slopes[part, t]
            half_row[t, :, rows] = lax.dot_general(
                col_mom[0, t], w, contract_last, preferred_element_type=jnp.float32
            )
            value = jnp.concatenate(
                [
                    jnp.dot(row_mom[i, t, :, rows], slopes[part, t, :, lanes], preferred_element_type=jnp.float32)
                    for lanes in (slice(0, half), slice(half, tile_size))
                ],
                axis=1,
            )
            if part == 0:
                half_col[t] = value
            else:
                half_col[t] += value

    def finish(n):
        _, i, _, local, exponent = place(n)
        scale = pick(exponent, SCALES) * (1.0 / tile_size)
        back = pick(exponent, [-0.5 / a for a in ALPHAS])
        moment, weight = gather_moments([half_row[0], half_row[1]])
        row_out[i] += fold(scale * (spread(row_ref[i]) * weight - back * moment))
        moment, weight = gather_moments([half_col[0], half_col[1]])
        col_out[local] += fold(scale * (spread(col_ref[local]) * weight - moment))

    def elementwise(n, part, uniform):
        n, i, column, _, exponent = place(n)
        slope = pick(exponent, SLOPES)
        first = column * tile_size
        if uniform:
            bins = first + lax.broadcasted_iota(jnp.int32, (8, tile_size), 1)
            same = (bins >= low_bin[i]) & (bins < high_bin[i])
            beta = jnp.where(same, BETA_SAME * slope, BETA_OTHER * slope)
            beta = jnp.concatenate([beta] * (STEP // 8), axis=0)
        else:
            row_chrom = chrom_row(starts, (row_first + n // slots) * tile_size + part * half, half).T[:, 0:1]
            col_chrom = chrom_row(starts, first, tile_size)[0:1]
        for c in range(half // STEP):
            rows = slice(c * STEP, (c + 1) * STEP)
            observed = counts[n, part * half + c * STEP : part * half + (c + 1) * STEP, :].astype(jnp.float32)
            if not uniform:
                beta = jnp.where(row_chrom[rows] == col_chrom, BETA_SAME * slope, BETA_OTHER * slope)
            for t in range(2):
                r = lax.rsqrt(dist[part, t, rows, :])
                r2 = r * r
                w = r2 * (observed - r2 * (r * (beta + r)))
                slopes[part, t, rows, :] = w.astype(jnp.bfloat16)

    def step(n, uniform):
        distances(n, 1)
        elementwise(n, 0, uniform)
        multiply(n - 1, 1)
        finish(n - 1)
        col_mom[0] = col_mom[1]
        prepare_column(n + 1)
        distances(n + 1, 0)
        elementwise(n, 1, uniform)
        multiply(n, 0)

    prepare_column(0)
    distances(0, 0)
    col_mom[0] = jnp.zeros_like(col_mom[1])

    def arrive(n):
        slot, i, _, _, _ = place(n)

        @pl.when(n < total)
        def _():
            copy(slot).wait()

        @pl.when(n + AHEAD < total)
        def _():
            copy(live[n + AHEAD]).start()

        return high_bin[i] >= (row_first + slot // slots + 1) * tile_size

    def general(n, carry):
        step(n, False)
        return carry

    def loop(n, carry):
        first = n * TOGETHER
        together = first + TOGETHER <= total
        for m in range(TOGETHER):
            together = together & arrive(first + m)

        @pl.when(together)
        def _():
            for m in range(TOGETHER):
                step(first + m, True)

        @pl.when(jnp.logical_not(together))
        def _():
            lax.fori_loop(first, jnp.minimum(first + TOGETHER, total), general, 0)

        return carry

    lax.fori_loop(0, (total + TOGETHER - 1) // TOGETHER, loop, 0)
    multiply(total - 1, 1)
    finish(total - 1)


def scratch_of(counts, rows):
    row_tiles, slots, tile_size = counts.shape[0], counts.shape[1], counts.shape[2]
    half = tile_size // 2
    return [
        pltpu.VMEM((row_tiles * slots, tile_size, tile_size), jnp.bfloat16),
        pltpu.SemaphoreType.DMA((row_tiles * slots,)),
        pltpu.SMEM((row_tiles * slots + 1,), jnp.int32),
        pltpu.SMEM((rows,), jnp.int32),
        pltpu.SMEM((rows,), jnp.int32),
        pltpu.VMEM((rows, 2, tile_size, 8 * GROUPS), jnp.bfloat16),
        pltpu.VMEM((rows, 2, MOMENTS, tile_size), jnp.bfloat16),
        pltpu.VMEM((2, 8 * GROUPS, tile_size), jnp.bfloat16),
        pltpu.VMEM((2, 2, MOMENTS, tile_size), jnp.bfloat16),
        pltpu.VMEM((2, 2, half, tile_size), jnp.bfloat16),
        pltpu.VMEM((2, 2, half, tile_size), jnp.float32),
        pltpu.VMEM((2, MOMENTS, tile_size), jnp.float32),
        pltpu.VMEM((2, MOMENTS, tile_size), jnp.float32),
    ]


SMEM = pl.BlockSpec(memory_space=pltpu.SMEM)
VMEM = pl.BlockSpec(memory_space=pltpu.VMEM)
PARAMS = pltpu.CompilerParams(vmem_limit_bytes=44 * 1024 * 1024)


def own_gradients(group, columns, exponents, starts, own_pos, counts):
    return pl.pallas_call(
        functools.partial(kernel, True),
        out_shape=jax.ShapeDtypeStruct(own_pos.shape, jnp.float32),
        in_specs=[SMEM] * 4 + [VMEM, pl.BlockSpec(memory_space=pl.ANY)],
        out_specs=VMEM,
        scratch_shapes=scratch_of(counts, own_pos.shape[0]),
        compiler_params=PARAMS,
        name="own_gradients",
    )(group, columns, exponents, starts, own_pos, counts)


def tile_gradients(group, columns, exponents, starts, row_pos, col_pos, counts):
    return pl.pallas_call(
        functools.partial(kernel, False),
        out_shape=[
            jax.ShapeDtypeStruct(row_pos.shape, jnp.float32),
            jax.ShapeDtypeStruct(col_pos.shape, jnp.float32),
        ],
        in_specs=[SMEM] * 4 + [VMEM] * 2 + [pl.BlockSpec(memory_space=pl.ANY)],
        out_specs=[VMEM, VMEM],
        scratch_shapes=scratch_of(counts, row_pos.shape[0]),
        compiler_params=PARAMS,
        name="tile_gradients",
    )(group, columns, exponents, starts, row_pos, col_pos, counts)


def body(coords, counts, tile_cols, exponents, chrom_starts):
    row_tiles, tile_size = counts.shape[0], counts.shape[2]
    width = coords.shape[2]
    tiles, quarters = width // tile_size, tile_size // LANES
    n_rows, n_cols = lax.axis_size(ROWS), lax.axis_size(COLS)
    local = coords.reshape(2, 3, tiles, quarters, LANES).transpose(2, 3, 0, 1, 4)
    local = local.reshape(tiles, 6 * quarters, LANES)
    col_pos = jnp.broadcast_to(local[None], (n_rows,) + local.shape)
    col_pos = lax.all_to_all(col_pos, ROWS, 0, 0, tiled=True).reshape((n_rows * tiles,) + local.shape[1:])
    pieces = [
        lax.ppermute(local, COLS, [((g + shift) % n_cols, g) for g in range(n_cols)]) for shift in range(1, n_cols)
    ]
    row_pos = jnp.concatenate([local] + pieces, axis=0)
    group = jnp.stack([lax.axis_index(ROWS), lax.axis_index(COLS), jnp.int32(n_cols)])
    own_part = own_gradients(group, tile_cols, exponents, chrom_starts, local, counts)
    row_part, col_part = tile_gradients(group, tile_cols, exponents, chrom_starts, row_pos, col_pos, counts)
    col_part = lax.all_to_all(col_part.reshape((n_rows,) + local.shape), ROWS, 0, 0, tiled=True)
    row_sum = own_part + row_part[:tiles]
    for shift in range(1, n_cols):
        piece = row_part[shift * tiles : (shift + 1) * tiles]
        row_sum += lax.ppermute(piece, COLS, [(g, (g + shift) % n_cols) for g in range(n_cols)])
    grad = jnp.sum(col_part, axis=0) + row_sum
    grad = grad.reshape(tiles, quarters, 2, 3, LANES).transpose(2, 3, 0, 1, 4)
    return grad.reshape(2, 3, width)


def solution(mesh):
    fine = Mesh(mesh.devices.reshape(2, 4, 4, 2, 2), ROWS + COLS)
    placed = (
        P(None, None, ROWS + COLS),
        P(ROWS, COLS, None, None),
        P(ROWS, COLS),
        P(ROWS, COLS),
        P(),
    )
    return jax.shard_map(
        body, mesh=fine, in_specs=placed, out_specs=P(None, None, ROWS + COLS), check_vma=False
    )
```
